32 devices in a mesh: replica: 2 (over x), fsdp: 16 (over z, y, core).
Axes of the slice: x: 2, y: 2, z: 4, core: 2. Of those that a mesh axis runs over, the one named last changes fastest.
Arguments:
- activations: bfloat16 [8192, 4096], P(('replica', 'fsdp')), may hold values from -6 to 6
- inner_weight: bfloat16 [2, 4096, 512], P('replica', 'fsdp'), may hold values from -0.09375 to 0.09375
- local_params: float32 [2, 2, 2, 4096, 512], P('replica', None, None, 'fsdp'), may hold values from -6 to 6
- base_params: float32 [2, 2, 4096, 512], P(None, None, 'fsdp'), may hold values from -6 to 6
- momentum: float32 [2, 2, 4096, 512], P(None, None, 'fsdp'), may hold values from -3 to 3
- inner_steps: int32 [2], P('replica'), may hold values from 16 to 72, as said below
Outputs:
- keys: bfloat16 [8192, 512], P(('replica', 'fsdp'))
- new_base: float32 [2, 2, 4096, 512], P(None, None, 'fsdp')
- new_momentum: float32 [2, 2, 4096, 512], P(None, None, 'fsdp')
The draws below stay inside these ranges and needn't reach their ends.
Inputs may be any that keep to these rules, and one draw needn't show every extreme that they name: `inner_steps`: some replica has done exactly 72 steps.
All inputs are finite; a program needn't handle non-finite values.
Results may differ from the reference program's by a relative error of at most 0.007.
Values may be sent and summed in bfloat16 or wider, within the bound.
No kernel may reach another device: no remote copies, remote signals or barrier semaphores. Data moves between devices by JAX's collectives and lax.ppermute only.
A program may use at most 64 MiB of HBM per device.

```python
import jax
import jax.numpy as jnp

DW = 4096
KV = 512
LAYERS = 2
REPLICAS = 2
TOKENS = 8192


def draw_inner_steps(key, part):
    key = jax.random.fold_in(key, 7)
    key_counts, key_place = jax.random.split(key)
    counts = jax.random.randint(key_counts, (REPLICAS,), 16, 73, dtype=jnp.int32)
    place = jax.random.randint(key_place, (), 0, REPLICAS, dtype=jnp.int32)
    ranks = jnp.arange(REPLICAS, dtype=jnp.int32)
    return jnp.where(ranks == place, 72, counts).astype(jnp.int32)


def block_levels(stream_key, extent, pieces, least, largest):
    def one(axis_at, blocks):
        heights = jax.random.uniform(jax.random.fold_in(jax.random.fold_in(stream_key, 6), axis_at), (blocks,), jnp.float32, least / len(pieces), largest / len(pieces))
        return jnp.repeat(jnp.exp(heights), extent[axis_at] // blocks).reshape((-1,) + (1,) * (len(extent) - axis_at - 1))

    loudness = one(*pieces[0])
    for cut in pieces[1:]:
        loudness = loudness * one(*cut)
    return loudness


def noise(own_key, shape, width, bound, cuts=(), held_as=jnp.bfloat16):
    gain = block_levels(own_key, shape, cuts, -0.22, 0.18) if cuts else 1.0
    array = jax.random.normal(own_key, shape, jnp.float32) * width * gain
    return jnp.minimum(jnp.maximum(array, -bound), bound).astype(held_as)


def setup_inputs(seed: int = 0) -> dict:
    seeds = jax.random.split(jax.random.key(seed), 7)
    activations = noise(seeds[0], (TOKENS, DW), 1.0, 6.0, ((0, 32),))
    inner_weight = noise(seeds[1], (REPLICAS, DW, KV), DW ** -0.5, 0.09375, ((0, 2), (1, 16)))
    local_params = noise(seeds[2], (REPLICAS, LAYERS, 2, DW, KV), 1.0, 6.0, ((0, 2), (3, 16)), jnp.float32)
    base_params = noise(seeds[3], (LAYERS, 2, DW, KV), 1.0, 6.0, ((2, 16),), jnp.float32)
    momentum = noise(seeds[4], (LAYERS, 2, DW, KV), 0.5, 3.0, ((2, 16),), jnp.float32)
    inner_steps = draw_inner_steps(jax.random.fold_in(seeds[6], 71), 0)
    return dict(activations=activations, inner_weight=inner_weight, local_params=local_params, base_params=base_params, momentum=momentum, inner_steps=inner_steps)


def reference(activations, inner_weight, local_params, base_params, momentum, inner_steps):
    rows = activations.shape[0] // REPLICAS
    blocks = []
    for group in range(REPLICAS):
        block = activations[group * rows:(group + 1) * rows]
        blocks.append(jnp.dot(block, inner_weight[group], preferred_element_type=jnp.float32).astype(jnp.bfloat16))
    keys = jnp.concatenate(blocks, axis=0)
    weights = inner_steps.astype(jnp.float32)
    summed = jnp.zeros(base_params.shape, jnp.float32)
    for group in range(REPLICAS):
        difference = (base_params - local_params[group]).astype(jnp.bfloat16)
        summed = summed + weights[group] * difference.astype(jnp.float32)
    average = summed / jnp.sum(weights)
    new_momentum = 0.9 * momentum + average
    new_base = base_params - 0.7 * (average + 0.9 * new_momentum)
    return keys, new_base, new_momentum
```

```python
import functools

import jax
import jax.numpy as jnp
from jax import lax
from jax.experimental import pallas as pl
from jax.experimental.pallas import tpu as pltpu
from jax.sharding import PartitionSpec as P

F32, BF16 = jnp.float32, jnp.bfloat16
MIB = 1024 * 1024
HBM = pl.BlockSpec(memory_space=pltpu.HBM)
VMEM = pl.BlockSpec(memory_space=pltpu.VMEM)


def nesterov(average, momentum, base_params):
    new_momentum = 0.9 * momentum + average
    new_base = base_params - 0.7 * (average + 0.9 * new_momentum)
    return (new_base, new_momentum)


def general(activations, inner_weight, local_params, base_params, momentum, inner_steps):
    counts = lax.all_gather(inner_steps, "replica", axis=0, tiled=True)
    total = jnp.sum(counts.astype(F32))
    own = inner_steps[0].astype(F32)
    difference = (base_params - local_params[0]).astype(BF16)
    average = lax.psum(own * difference.astype(F32), "replica") / total
    new_base, new_momentum = nesterov(average, momentum, base_params)
    weight = lax.all_gather(inner_weight[0], "fsdp", axis=0, tiled=True)
    keys = jnp.dot(activations, weight, preferred_element_type=F32).astype(BF16)
    return (keys, new_base, new_momentum)


def index(z, y, c):
    return (z * 2 + y) * 2 + c


def place(p):
    p = p % 8
    return (p, 0) if p < 4 else (7 - p, 1)


def cycle(x, by):
    pairs = [
        (index(*place(p), c), index(*place(p + by), c)) for p in range(8) for c in range(2)
    ]
    return lax.ppermute(x, "fsdp", pairs)


def up(x):
    return cycle(x, 1)


def down(x):
    return cycle(x, -1)


def send_core(x):
    pairs = [(i, i ^ 1) for i in range(16)]
    return lax.ppermute(x, "fsdp", pairs)


def send_x(x):
    return lax.ppermute(x, "replica", [(0, 1), (1, 0)])


def tie(*xs):
    return lax.optimization_barrier(xs)


def cost(flops, bytes_accessed):
    return pl.CostEstimate(flops=int(flops), bytes_accessed=int(bytes_accessed), transcendentals=0)


def params(limit=16):
    return pltpu.CompilerParams(vmem_limit_bytes=limit * MIB)


def difference_kernel(pieces, base, local, steps, out, count, held, sems):
    rows = base.shape[0]
    piece = rows // pieces
    copies = []
    for j in range(pieces):
        for i, ref in enumerate((base, local)):
            at = pl.ds(j * piece, piece)
            copies.append(pltpu.make_async_copy(ref.at[at, :], held.at[i, at, :], sems.at[i, j]))
    load = pltpu.make_async_copy(steps, count, sems.at[0, pieces])
    for copy in copies:
        copy.start()
    load.start()
    for j in range(pieces):
        copies[2 * j].wait()
        copies[2 * j + 1].wait()
        at = pl.ds(j * piece, piece)
        out[at, :] = (held[0, at, :] - held[1, at, :]).astype(BF16)
    load.wait()
    extra = out.shape[0] - rows
    out[pl.ds(rows, extra), :] = jnp.full((extra, out.shape[1]), count[0].astype(F32), F32).astype(BF16)


def difference(base, local, steps):
    rows, width = base.shape
    pieces = 4
    return pl.pallas_call(
        functools.partial(difference_kernel, pieces),
        out_shape=jax.ShapeDtypeStruct((rows + 16, width), BF16),
        in_specs=[HBM, HBM, HBM],
        out_specs=pl.BlockSpec(memory_space=pltpu.VMEM),
        scratch_shapes=[
            pltpu.SMEM((1,), jnp.int32),
            pltpu.VMEM((2, rows, width), F32),
            pltpu.SemaphoreType.DMA((2, pieces + 1)),
        ],
        compiler_params=params(52),
        cost_estimate=cost(2 * rows * width, 10 * rows * width),
        name="difference",
    )(base, local, steps)


def outer_kernel(pieces, base, mom, own, got, new_base, new_mom, held, sems):
    rows = base.shape[0]
    piece = rows // pieces
    mine = own[pl.ds(rows, 16), :][0:1, :].astype(F32)
    theirs = got[pl.ds(rows, 16), :][0:1, :].astype(F32)
    scale = 1.0 / (mine + theirs)
    mine, theirs = mine * scale, theirs * scale
    copies = []
    for j in range(pieces):
        at = pl.ds(j * piece, piece)
        average = mine * own[at, :].astype(F32) + theirs * got[at, :].astype(F32)
        momentum = 0.9 * mom[at, :] + average
        held[1, at, :] = momentum
        held[0, at, :] = base[at, :] - 0.7 * (average + 0.9 * momentum)
        for i, ref in enumerate((new_base, new_mom)):
            copies.append(pltpu.make_async_copy(held.at[i, at, :], ref.at[at, :], sems.at[i, j]))
            copies[-1].start()
    for copy in copies:
        copy.wait()


def outer(base, mom, own, got):
    rows, width = base.shape
    pieces = 8
    shape = jax.ShapeDtypeStruct(base.shape, F32)
    return pl.pallas_call(
        functools.partial(outer_kernel, pieces),
        out_shape=(shape, shape),
        in_specs=[VMEM] * 4,
        out_specs=(HBM, HBM),
        scratch_shapes=[pltpu.VMEM((2, rows, width), F32), pltpu.SemaphoreType.DMA((2, pieces))],
        compiler_params=params(),
        cost_estimate=cost(10 * rows * width, 20 * rows * width),
        name="outer_step",
    )(base, mom, own, got)


def dot(a, b):
    return jnp.dot(a, b, preferred_element_type=F32)


def column(by, mine, depth):
    f = lax.axis_index("fsdp")
    z, y, c = f // 4, (f // 2) % 2, f % 2
    p = (z + y * (7 - 2 * z) + by + 8) % 8
    far = p // 4
    z, y = p + far * (7 - 2 * p), far
    c = c if mine else 1 - c
    return pl.multiple_of(index(z, y, c) * depth, depth)


def partial_kernel(places, whole, first, act, sib, *refs):
    n = len(places)
    refs, (own_out, sib_out) = refs[:-2], refs[-2:]
    parts = 1 if whole else 2
    weights, state = refs[:-2] if not first else refs, refs[-2:]
    depth = act.shape[1] // 16
    own = None if first else state[0][...]
    theirs = None if first else state[1][...]
    at = 0
    for by in places:
        if by == 0:
            w = weights[at][...]
            at += 1
        else:
            w = jnp.concatenate([weights[at][...], weights[at + 1][...]], axis=0)
            at += 2
        columns = pl.ds(column(by, True, depth), depth)
        a, b = dot(act[:, columns], w), dot(sib[:, columns], w)
        own = a if own is None else own + a
        theirs = b if theirs is None else theirs + b
    own_out[...] = own
    sib_out[...] = theirs


def partial_sums(places, act, sib, weights, state):
    tokens = act.shape[0]
    width = weights[0].shape[1]
    out = jax.ShapeDtypeStruct((tokens, width), F32)
    return pl.pallas_call(
        functools.partial(partial_kernel, places, False, not state),
        out_shape=(out, out),
        in_specs=[VMEM] * (2 + len(weights) + len(state)),
        out_specs=(VMEM, VMEM),
        compiler_params=params(),
        cost_estimate=cost(0, 0),
        name="partial_keys",
    )(act, sib, *weights, *state)


def finish_kernel(act, wa, wb, va, vb, own, got, keys):
    half = wa.shape[0]
    depth = 2 * half
    total = own[...] + got[...]
    for mine, a, b in ((True, wa, wb), (False, va, vb)):
        w = jnp.concatenate([a[...], b[...]], axis=0)
        total += dot(act[:, pl.ds(column(4, mine, depth), depth)], w)
    keys[...] = total.astype(BF16)


def finish(act, wa, wb, va, vb, own, got):
    tokens, width = own.shape
    return pl.pallas_call(
        finish_kernel,
        out_shape=jax.ShapeDtypeStruct((tokens, width), BF16),
        in_specs=[VMEM] * 7,
        out_specs=VMEM,
        compiler_params=params(),
        cost_estimate=cost(0, 0),
        name="finish_keys",
    )(act, wa, wb, va, vb, own, got)


def special(activations, inner_weight, local_params, base_params, momentum, inner_steps):
    shape = base_params.shape
    flat = lambda a: a.reshape(-1, shape[-1])
    base, mom, local = flat(base_params), flat(momentum), flat(local_params)
    w = inner_weight[0]
    half = w.shape[0] // 2

    own = difference(base, local, inner_steps)
    got = send_x(own)
    sib = send_core(activations)

    w = tie(w, own)[0]
    wa, wb = w[:half], w[half:]
    ua, da = [up(wa)], [down(wa)]
    wb = tie(wb, sib)[0]
    ub, db = [up(wb)], [down(wb)]
    for _ in range(2):
        ua.append(up(ua[-1]))
        da.append(down(da[-1]))
        ub.append(up(ub[-1]))
        db.append(down(db[-1]))
    state = partial_sums(
        (0, -1, 1, -2, 2), activations, sib,
        (w, ua[0], ub[0], da[0], db[0], ua[1], ub[1], da[1], db[1]), (),
    )
    ua4, db4 = up(ua[2]), down(db[2])
    state = partial_sums((-3, 3), activations, sib, (ua[2], ub[2], da[2], db[2]), state)
    swapped = send_core(state[1])

    ua4, db4, swapped, got = tie(ua4, db4, swapped, got)
    va, vb = send_core(ua4), send_core(db4)
    keys = finish(activations, ua4, db4, va, vb, state[0], swapped)
    new = outer(base, mom, own, got)
    return (keys, new[0].reshape(shape), new[1].reshape(shape))


def solution(mesh):
    fast = mesh.shape["replica"] == 2 and mesh.shape["fsdp"] == 16
    return jax.shard_map(
        special if fast else general,
        mesh=mesh,
        in_specs=(
            P(("replica", "fsdp"), None),
            P("replica", "fsdp", None),
            P("replica", None, None, "fsdp", None),
            P(None, None, "fsdp", None),
            P(None, None, "fsdp", None),
            P("replica"),
        ),
        out_specs=(
            P(("replica", "fsdp"), None),
            P(None, None, "fsdp", None),
            P(None, None, "fsdp", None),
        ),
        check_vma=False,
    )
```

```python
import functools

import jax
import jax.numpy as jnp
from jax import lax
from jax.experimental import pallas as pl
from jax.experimental.pallas import tpu as pltpu
from jax.sharding import PartitionSpec as P

F32, BF16 = jnp.float32, jnp.bfloat16
MIB = 1024 * 1024
HBM = pl.BlockSpec(memory_space=pltpu.HBM)
VMEM = pl.BlockSpec(memory_space=pltpu.VMEM)


def nesterov(average, momentum, base_params):
    new_momentum = 0.9 * momentum + average
    new_base = base_params - 0.7 * (average + 0.9 * new_momentum)
    return (new_base, new_momentum)


def general(activations, inner_weight, local_params, base_params, momentum, inner_steps):
    counts = lax.all_gather(inner_steps, "replica", axis=0, tiled=True)
    total = jnp.sum(counts.astype(F32))
    own = inner_steps[0].astype(F32)
    difference = (base_params - local_params[0]).astype(BF16)
    average = lax.psum(own * difference.astype(F32), "replica") / total
    new_base, new_momentum = nesterov(average, momentum, base_params)
    weight = lax.all_gather(inner_weight[0], "fsdp", axis=0, tiled=True)
    keys = jnp.dot(activations, weight, preferred_element_type=F32).astype(BF16)
    return (keys, new_base, new_momentum)


def index(z, y, c):
    return (z * 2 + y) * 2 + c


def place(p):
    p = p % 8
    return (p, 0) if p < 4 else (7 - p, 1)


def cycle(x, by):
    pairs = [
        (index(*place(p), c), index(*place(p + by), c)) for p in range(8) for c in range(2)
    ]
    return lax.ppermute(x, "fsdp", pairs)


def up(x):
    return cycle(x, 1)


def down(x):
    return cycle(x, -1)


def send_core(x):
    pairs = [(i, i ^ 1) for i in range(16)]
    return lax.ppermute(x, "fsdp", pairs)


def send_x(x):
    return lax.ppermute(x, "replica", [(0, 1), (1, 0)])


def tie(*xs):
    return lax.optimization_barrier(xs)


def cost(flops, bytes_accessed):
    return pl.CostEstimate(flops=int(flops), bytes_accessed=int(bytes_accessed), transcendentals=0)


def params(limit=16):
    return pltpu.CompilerParams(vmem_limit_bytes=limit * MIB)


def difference_kernel(pieces, base, local, steps, out, held, sems):
    rows = base.shape[0]
    piece = rows // pieces
    copies = []
    for j in range(pieces):
        for i, ref in enumerate((base, local)):
            at = pl.ds(j * piece, piece)
            copies.append(pltpu.make_async_copy(ref.at[at, :], held.at[i, at, :], sems.at[i, j]))

    for copy in copies:
        copy.start()
    for j in range(pieces):
        copies[2 * j].wait()
        copies[2 * j + 1].wait()
        at = pl.ds(j * piece, piece)
        out[at, :] = (held[0, at, :] - held[1, at, :]).astype(BF16)
    extra = out.shape[0] - rows
    out[pl.ds(rows, extra), :] = jnp.broadcast_to(steps[...].astype(F32), (extra, out.shape[1])).astype(BF16)


def difference(base, local, steps):
    rows, width = base.shape
    pieces = 4
    return pl.pallas_call(
        functools.partial(difference_kernel, pieces),
        out_shape=jax.ShapeDtypeStruct((rows + 16, width), BF16),
        in_specs=[HBM, HBM, VMEM],
        out_specs=pl.BlockSpec(memory_space=pltpu.VMEM),
        scratch_shapes=[
            pltpu.VMEM((2, rows, width), F32),
            pltpu.SemaphoreType.DMA((2, pieces)),
        ],
        compiler_params=params(52),
        cost_estimate=cost(2 * rows * width, 10 * rows * width),
        name="difference",
    )(base, local, steps.reshape(1, 1))


def outer_kernel(pieces, base, mom, own, got, new_base, new_mom, held, sems):
    rows = base.shape[0]
    piece = rows // pieces
    mine = own[pl.ds(rows, 16), :][0:1, :].astype(F32)
    theirs = got[pl.ds(rows, 16), :][0:1, :].astype(F32)
    scale = 1.0 / (mine + theirs)
    mine, theirs = mine * scale, theirs * scale
    copies = []
    for j in range(pieces):
        at = pl.ds(j * piece, piece)
        average = mine * own[at, :].astype(F32) + theirs * got[at, :].astype(F32)
        momentum = 0.9 * mom[at, :] + average
        held[1, at, :] = momentum
        held[0, at, :] = base[at, :] - 0.7 * (average + 0.9 * momentum)
        for i, ref in enumerate((new_base, new_mom)):
            copies.append(pltpu.make_async_copy(held.at[i, at, :], ref.at[at, :], sems.at[i, j]))
            copies[-1].start()
    for copy in copies:
        copy.wait()


def outer(base, mom, own, got):
    rows, width = base.shape
    pieces = 8
    shape = jax.ShapeDtypeStruct(base.shape, F32)
    return pl.pallas_call(
        functools.partial(outer_kernel, pieces),
        out_shape=(shape, shape),
        in_specs=[VMEM] * 4,
        out_specs=(HBM, HBM),
        scratch_shapes=[pltpu.VMEM((2, rows, width), F32), pltpu.SemaphoreType.DMA((2, pieces))],
        compiler_params=params(),
        cost_estimate=cost(10 * rows * width, 20 * rows * width),
        name="outer_step",
    )(base, mom, own, got)


def dot(a, b):
    return jnp.dot(a, b, preferred_element_type=F32)


def column(by, mine, depth):
    f = lax.axis_index("fsdp")
    z, y, c = f // 4, (f // 2) % 2, f % 2
    p = (z + y * (7 - 2 * z) + by + 8) % 8
    far = p // 4
    z, y = p + far * (7 - 2 * p), far
    c = c if mine else 1 - c
    return pl.multiple_of(index(z, y, c) * depth, depth)


def partial_kernel(places, whole, first, act, sib, *refs):
    n = len(places)
    refs, (own_out, sib_out) = refs[:-2], refs[-2:]
    parts = 1 if whole else 2
    weights, state = refs[:-2] if not first else refs, refs[-2:]
    depth = act.shape[1] // 16
    own = None if first else state[0][...]
    theirs = None if first else state[1][...]
    at = 0
    for by in places:
        if by == 0:
            w = weights[at][...]
            at += 1
        else:
            w = jnp.concatenate([weights[at][...], weights[at + 1][...]], axis=0)
            at += 2
        columns = pl.ds(column(by, True, depth), depth)
        a, b = dot(act[:, columns], w), dot(sib[:, columns], w)
        own = a if own is None else own + a
        theirs = b if theirs is None else theirs + b
    own_out[...] = own
    sib_out[...] = theirs.astype(sib_out.dtype)


def partial_sums(places, act, sib, weights, state, kind=F32):
    tokens = act.shape[0]
    width = weights[0].shape[1]
    out = jax.ShapeDtypeStruct((tokens, width), F32)
    return pl.pallas_call(
        functools.partial(partial_kernel, places, False, not state),
        out_shape=(out, jax.ShapeDtypeStruct((tokens, width), kind)),
        in_specs=[VMEM] * (2 + len(weights) + len(state)),
        out_specs=(VMEM, VMEM),
        compiler_params=params(),
        cost_estimate=cost(0, 0),
        name="partial_keys",
    )(act, sib, *weights, *state)


def finish_kernel(act, wa, wb, va, vb, own, got, keys):
    half = wa.shape[0]
    depth = 2 * half
    total = own[...] + got[...].astype(F32)
    for mine, a, b in ((True, wa, wb), (False, va, vb)):
        w = jnp.concatenate([a[...], b[...]], axis=0)
        total += dot(act[:, pl.ds(column(4, mine, depth), depth)], w)
    keys[...] = total.astype(BF16)


def finish(act, wa, wb, va, vb, own, got):
    tokens, width = own.shape
    return pl.pallas_call(
        finish_kernel,
        out_shape=jax.ShapeDtypeStruct((tokens, width), BF16),
        in_specs=[VMEM] * 7,
        out_specs=VMEM,
        compiler_params=params(),
        cost_estimate=cost(0, 0),
        name="finish_keys",
    )(act, wa, wb, va, vb, own, got)


def special(activations, inner_weight, local_params, base_params, momentum, inner_steps):
    shape = base_params.shape
    flat = lambda a: a.reshape(-1, shape[-1])
    base, mom, local = flat(base_params), flat(momentum), flat(local_params)
    w = inner_weight[0]
    half = w.shape[0] // 2

    own = difference(base, local, inner_steps)
    got = send_x(own)
    sib = send_core(activations)

    w = tie(w, own)[0]
    wa, wb = w[:half], w[half:]
    ua, da = [up(wa)], [down(wa)]
    wb = tie(wb, sib)[0]
    ub, db = [up(wb)], [down(wb)]
    ua.append(up(ua[0]))
    da.append(down(da[0]))
    ub.append(up(ub[0]))
    db.append(down(db[0]))
    state = partial_sums((0, -1, 1), activations, sib, (w, ua[0], ub[0], da[0], db[0]), ())
    ua[1], da[1], *state = tie(ua[1], da[1], *state)
    ua.append(up(ua[1]))
    da.append(down(da[1]))
    ub.append(up(ub[1]))
    db.append(down(db[1]))
    state = partial_sums((-2, 2), activations, sib, (ua[1], ub[1], da[1], db[1]), state)
    ua[2], db[2], *state = tie(ua[2], db[2], *state)
    ua4, db4 = up(ua[2]), down(db[2])
    own_sum, sib_sum = partial_sums((-3, 3), activations, sib, (ua[2], ub[2], da[2], db[2]), state, BF16)
    swapped = send_core(sib_sum)
    got, own_sum = tie(got, own_sum)
    new = outer(base, mom, own, got)
    ua4, db4, *new = tie(ua4, db4, *new)
    va, vb = send_core(ua4), send_core(db4)
    keys = finish(activations, ua4, db4, va, vb, own_sum, swapped)
    return (keys, new[0].reshape(shape), new[1].reshape(shape))


def solution(mesh):
    fast = mesh.shape["replica"] == 2 and mesh.shape["fsdp"] == 16
    return jax.shard_map(
        special if fast else general,
        mesh=mesh,
        in_specs=(
            P(("replica", "fsdp"), None),
            P("replica", "fsdp", None),
            P("replica", None, None, "fsdp", None),
            P(None, None, "fsdp", None),
            P(None, None, "fsdp", None),
            P("replica"),
        ),
        out_specs=(
            P(("replica", "fsdp"), None),
            P(None, None, "fsdp", None),
            P(None, None, "fsdp", None),
        ),
        check_vma=False,
    )
```

```python
import functools

import jax
import jax.numpy as jnp
from jax import lax
from jax.experimental import pallas as pl
from jax.experimental.pallas import tpu as pltpu
from jax.sharding import PartitionSpec as P

F32, BF16 = jnp.float32, jnp.bfloat16
MIB = 1024 * 1024
HBM = pl.BlockSpec(memory_space=pltpu.HBM)
ANY = pl.BlockSpec(memory_space=pl.ANY)
VMEM = pl.BlockSpec(memory_space=pltpu.VMEM)


def nesterov(average, momentum, base_params):
    new_momentum = 0.9 * momentum + average
    new_base = base_params - 0.7 * (average + 0.9 * new_momentum)
    return (new_base, new_momentum)


def general(activations, inner_weight, local_params, base_params, momentum, inner_steps):
    counts = lax.all_gather(inner_steps, "replica", axis=0, tiled=True)
    total = jnp.sum(counts.astype(F32))
    own = inner_steps[0].astype(F32)
    difference = (base_params - local_params[0]).astype(BF16)
    average = lax.psum(own * difference.astype(F32), "replica") / total
    new_base, new_momentum = nesterov(average, momentum, base_params)
    weight = lax.all_gather(inner_weight[0], "fsdp", axis=0, tiled=True)
    keys = jnp.dot(activations, weight, preferred_element_type=F32).astype(BF16)
    return (keys, new_base, new_momentum)


def index(z, y, c):
    return (z * 2 + y) * 2 + c


def place(p):
    p = p % 8
    return (p, 0) if p < 4 else (7 - p, 1)


def cycle(x):
    pairs = [
        (index(*place(p), c), index(*place(p + 1 - 2 * c), c)) for p in range(8) for c in range(2)
    ]
    return lax.ppermute(x, "fsdp", pairs)


def send_core(x):
    pairs = [(i, i ^ 1) for i in range(16)]
    return lax.ppermute(x, "fsdp", pairs)


def send_x(x):
    return lax.ppermute(x, "replica", [(0, 1), (1, 0)])


def tie(*xs):
    return lax.optimization_barrier(xs)


def cost(flops, bytes_accessed):
    return pl.CostEstimate(flops=int(flops), bytes_accessed=int(bytes_accessed), transcendentals=0)


def params(limit=16):
    return pltpu.CompilerParams(vmem_limit_bytes=limit * MIB)


def difference_kernel(at, sizes, pieces, base, local, *refs):
    held, sems = refs[-2:]
    outs = refs[-2 - len(sizes):-2]
    rows = held.shape[1]
    piece = rows // pieces
    copies = []
    for j in range(pieces):
        for i, ref in enumerate((base, local)):
            part = pl.ds(j * piece, piece)
            copies.append(
                pltpu.make_async_copy(ref.at[pl.ds(at + j * piece, piece), :], held.at[i, part, :], sems.at[i, j])
            )
    for copy in copies:
        copy.start()
    extra = outs[0].shape[0] - sizes[0]
    if extra:
        count = jnp.broadcast_to(refs[0][...].astype(F32), (extra, outs[0].shape[1]))
        outs[0][pl.ds(sizes[0], extra), :] = count.astype(BF16)
    which, put = 0, 0
    for j in range(pieces):
        copies[2 * j].wait()
        copies[2 * j + 1].wait()
        part = pl.ds(j * piece, piece)
        outs[which][pl.ds(put, piece), :] = (held[0, part, :] - held[1, part, :]).astype(BF16)
        put += piece
        if put == sizes[which]:
            which, put = which + 1, 0


def difference(base, local, at, sizes, pieces, steps=()):
    width = base.shape[1]
    rows = sum(sizes)
    shapes = [jax.ShapeDtypeStruct((n, width), BF16) for n in sizes]
    if steps:
        shapes[0] = jax.ShapeDtypeStruct((sizes[0] + 16, width), BF16)
    return pl.pallas_call(
        functools.partial(difference_kernel, at, tuple(sizes), pieces),
        out_shape=tuple(shapes),
        in_specs=[HBM, HBM] + [VMEM] * len(steps),
        out_specs=(VMEM,) * len(sizes),
        scratch_shapes=[pltpu.VMEM((2, rows, width), F32), pltpu.SemaphoreType.DMA((2, pieces))],
        compiler_params=params(52),
        cost_estimate=cost(2 * rows * width, 10 * rows * width),
        name="difference",
    )(base, local, *steps)


def outer_kernel(base, mom, own, got, mine, theirs, *refs):
    new_base, new_mom = refs[-2:]
    mine = mine[...][0:1, :].astype(F32)
    theirs = theirs[...][0:1, :].astype(F32)
    scale = 1.0 / (mine + theirs)
    average = (mine * scale) * own[...].astype(F32) + (theirs * scale) * got[...].astype(F32)
    momentum = 0.9 * mom[...] + average
    new_mom[...] = momentum
    new_base[...] = base[...] - 0.7 * (average + 0.9 * momentum)


def outer(base, mom, own, got, mine, theirs, at, rows, block, state):
    width = own.shape[1]
    big = pl.BlockSpec((pl.Element(block), pl.Element(width)), lambda i: (pl.multiple_of(at + i * block, 16), 0))
    small = pl.BlockSpec((block, width), lambda i: (i, 0))
    counts = mine.shape[0] // 16 - 1
    steps = pl.BlockSpec((16, width), lambda i: (counts, 0))
    shape = jax.ShapeDtypeStruct(base.shape, F32)
    return pl.pallas_call(
        outer_kernel,
        out_shape=(shape, shape),
        grid=(rows // block,),
        in_specs=[big, big, small, small, steps, steps] + [ANY] * len(state),
        out_specs=(big, big),
        input_output_aliases={6 + i: i for i in range(len(state))},
        compiler_params=params(),
        cost_estimate=cost(10 * rows * width, 20 * rows * width),
        name="outer_step",
    )(base, mom, own, got, mine, theirs, *state)


def dot(a, b):
    return jnp.dot(a, b, preferred_element_type=F32)


def column(back, mine, depth):
    f = lax.axis_index("fsdp")
    z, y, c = f // 4, (f // 2) % 2, f % 2
    p = (z + y * (7 - 2 * z) - back * (1 - 2 * c) + 8) % 8
    far = p // 4
    z, y = p + far * (7 - 2 * p), far
    c = c if mine else 1 - c
    return pl.multiple_of(index(z, y, c) * depth, depth)


def partial_kernel(blocks, first, act, sib, *refs):
    refs, (own_out, sib_out) = refs[:-2], refs[-2:]
    weights, state = (refs, None) if first else (refs[:-2], refs[-2:])
    depth = act.shape[1] // 16
    own = None if first else state[0][...]
    theirs = None if first else state[1][...]
    for (back, mine), ref in zip(blocks, weights):
        w = ref[...]
        columns = pl.ds(column(back, mine, depth), depth)
        a, b = dot(act[:, columns], w), dot(sib[:, columns], w)
        own = a if own is None else own + a
        theirs = b if theirs is None else theirs + b
    own_out[...] = own
    sib_out[...] = theirs.astype(sib_out.dtype)


def partial_sums(blocks, act, sib, weights, state, kind=F32):
    tokens = act.shape[0]
    width = weights[0].shape[1]
    out = jax.ShapeDtypeStruct((tokens, width), F32)
    return pl.pallas_call(
        functools.partial(partial_kernel, blocks, not state),
        out_shape=(out, jax.ShapeDtypeStruct((tokens, width), kind)),
        in_specs=[VMEM] * (2 + len(weights) + len(state)),
        out_specs=(VMEM, VMEM),
        compiler_params=params(),
        cost_estimate=cost(0, 0),
        name="partial_keys",
    )(act, sib, *weights, *state)


def close_kernel(at, act, mine, other, own, got, base, mom, diff, sent, steps0, steps1, *refs):
    keys, new_base, new_mom, loaded, stored, done, sems = refs[-7:]
    rows = diff.shape[0]
    part = pl.ds(at, rows)
    loads = [
        pltpu.make_async_copy(ref.at[part, :], loaded.at[i], sems.at[i]) for i, ref in enumerate((base, mom))
    ]
    for copy in loads:
        copy.start()
    depth = mine.shape[0]
    total = own[...] + got[...].astype(F32)
    total += dot(act[:, pl.ds(column(4, True, depth), depth)], mine[...])
    total += dot(act[:, pl.ds(column(4, False, depth), depth)], other[...])
    done[...] = total.astype(BF16)
    stores = [pltpu.make_async_copy(done, keys, sems.at[2])]
    stores[0].start()
    n = steps0.shape[0]
    ours = steps0[pl.ds(n - 16, 16), :][0:1, :].astype(F32)
    theirs = steps1[pl.ds(n - 16, 16), :][0:1, :].astype(F32)
    scale = 1.0 / (ours + theirs)
    average = (ours * scale) * diff[...].astype(F32) + (theirs * scale) * sent[...].astype(F32)
    for copy in loads:
        copy.wait()
    momentum = 0.9 * loaded[1] + average
    stored[1] = momentum
    stored[0] = loaded[0] - 0.7 * (average + 0.9 * momentum)
    for i, ref in enumerate((new_base, new_mom)):
        stores.append(pltpu.make_async_copy(stored.at[i], ref.at[part, :], sems.at[3 + i]))
        stores[-1].start()
    for copy in stores:
        copy.wait()


def close(act, mine, other, own, got, base, mom, diff, sent, steps0, steps1, at, state):
    tokens, width = own.shape
    rows = diff.shape[0]
    shape = jax.ShapeDtypeStruct(base.shape, F32)
    return pl.pallas_call(
        functools.partial(close_kernel, at),
        out_shape=(jax.ShapeDtypeStruct((tokens, width), BF16), shape, shape),
        in_specs=[VMEM] * 5 + [ANY] * 2 + [VMEM] * 4 + [ANY] * 2,
        out_specs=(ANY, ANY, ANY),
        input_output_aliases={11: 1, 12: 2},
        scratch_shapes=[
            pltpu.VMEM((2, rows, width), F32),
            pltpu.VMEM((2, rows, width), F32),
            pltpu.VMEM((tokens, width), BF16),
            pltpu.SemaphoreType.DMA((5,)),
        ],
        compiler_params=params(),
        cost_estimate=cost(0, 0),
        name="close",
    )(act, mine, other, own, got, base, mom, diff, sent, steps0, steps1, *state)


def special(activations, inner_weight, local_params, base_params, momentum, inner_steps):
    shape = base_params.shape
    flat = lambda a: a.reshape(-1, shape[-1])
    base, mom, local = flat(base_params), flat(momentum), flat(local_params)
    w = inner_weight[0]

    rows = base.shape[0]
    n1 = rows * 4 // 16
    n0 = rows - n1
    sib = send_core(activations)
    own0, own1 = difference(base, local, 0, (n0, n1), 4, (inner_steps.reshape(1, 1),))
    got0, got1 = send_x(own0), send_x(own1)
    w = tie(w, own0)[0]
    a1 = cycle(w)
    wsib = send_core(w)
    b1 = cycle(tie(wsib, sib)[0])
    a2 = cycle(a1)
    b2 = cycle(b1)
    state = partial_sums(((0, True), (1, True), (1, False)), activations, sib, (w, a1, b1), ())
    a2, *state = tie(a2, *state)
    a3 = cycle(a2)
    b3 = cycle(b2)
    state = partial_sums(((2, True), (2, False)), activations, sib, (a2, b2), state)
    a3, *state = tie(a3, *state)
    last = cycle(a3)
    own_sum, sib_sum = partial_sums(((3, True), (3, False)), activations, sib, (a3, b3), state, BF16)
    swapped = send_core(sib_sum)
    got0, own_sum = tie(got0, own_sum)
    new = outer(base, mom, own0, got0, own0, got0, 0, n0, n0 // 2, ())
    last, *new = tie(last, *new)
    other = send_core(last)
    keys, *new = close(
        activations, last, other, own_sum, swapped, base, mom, own1, got1, own0, got0, n0, new
    )
    return (keys, new[0].reshape(shape), new[1].reshape(shape))


def solution(mesh):
    fast = mesh.shape["replica"] == 2 and mesh.shape["fsdp"] == 16
    return jax.shard_map(
        special if fast else general,
        mesh=mesh,
        in_specs=(
            P(("replica", "fsdp"), None),
            P("replica", "fsdp", None),
            P("replica", None, None, "fsdp", None),
            P(None, None, "fsdp", None),
            P(None, None, "fsdp", None),
            P("replica"),
        ),
        out_specs=(
            P(("replica", "fsdp"), None),
            P(None, None, "fsdp", None),
            P(None, None, "fsdp", None),
        ),
        check_vma=False,
    )
```

```python
import functools

import jax
import jax.numpy as jnp
from jax import lax
from jax.experimental import pallas as pl
from jax.experimental.pallas import tpu as pltpu
from jax.sharding import PartitionSpec as P

F32, BF16 = jnp.float32, jnp.bfloat16
MIB = 1024 * 1024
HBM = pl.BlockSpec(memory_space=pltpu.HBM)
ANY = pl.BlockSpec(memory_space=pl.ANY)
VMEM = pl.BlockSpec(memory_space=pltpu.VMEM)


def nesterov(average, momentum, base_params):
    new_momentum = 0.9 * momentum + average
    new_base = base_params - 0.7 * (average + 0.9 * new_momentum)
    return (new_base, new_momentum)


def general(activations, inner_weight, local_params, base_params, momentum, inner_steps):
    counts = lax.all_gather(inner_steps, "replica", axis=0, tiled=True)
    total = jnp.sum(counts.astype(F32))
    own = inner_steps[0].astype(F32)
    difference = (base_params - local_params[0]).astype(BF16)
    average = lax.psum(own * difference.astype(F32), "replica") / total
    new_base, new_momentum = nesterov(average, momentum, base_params)
    weight = lax.all_gather(inner_weight[0], "fsdp", axis=0, tiled=True)
    keys = jnp.dot(activations, weight, preferred_element_type=F32).astype(BF16)
    return (keys, new_base, new_momentum)


def index(z, y, c):
    return (z * 2 + y) * 2 + c


def place(p):
    p = p % 8
    return (p, 0) if p < 4 else (7 - p, 1)


def cycle(x):
    pairs = [
        (index(*place(p), c), index(*place(p + 1 - 2 * c), c)) for p in range(8) for c in range(2)
    ]
    return lax.ppermute(x, "fsdp", pairs)


def send_core(x):
    pairs = [(i, i ^ 1) for i in range(16)]
    return lax.ppermute(x, "fsdp", pairs)


def send_x(x):
    return lax.ppermute(x, "replica", [(0, 1), (1, 0)])


def tie(*xs):
    return lax.optimization_barrier(xs)


def cost(flops, bytes_accessed):
    return pl.CostEstimate(flops=int(flops), bytes_accessed=int(bytes_accessed), transcendentals=0)


def params(limit=16):
    return pltpu.CompilerParams(vmem_limit_bytes=limit * MIB)


def difference_kernel(at, sizes, pieces, base, local, *refs):
    held, sems = refs[-2:]
    outs = refs[-2 - len(sizes):-2]
    rows = held.shape[1]
    piece = rows // pieces
    copies = []
    for j in range(pieces):
        for i, ref in enumerate((base, local)):
            part = pl.ds(j * piece, piece)
            copies.append(
                pltpu.make_async_copy(ref.at[pl.ds(at + j * piece, piece), :], held.at[i, part, :], sems.at[i, j])
            )
    for copy in copies:
        copy.start()
    extra = outs[0].shape[0] - sizes[0]
    if extra:
        count = jnp.broadcast_to(refs[0][...].astype(F32), (extra, outs[0].shape[1]))
        outs[0][pl.ds(sizes[0], extra), :] = count.astype(BF16)
    which, put = 0, 0
    for j in range(pieces):
        copies[2 * j].wait()
        copies[2 * j + 1].wait()
        part = pl.ds(j * piece, piece)
        outs[which][pl.ds(put, piece), :] = (held[0, part, :] - held[1, part, :]).astype(BF16)
        put += piece
        if put == sizes[which]:
            which, put = which + 1, 0


def difference(base, local, at, sizes, pieces, steps=()):
    width = base.shape[1]
    rows = sum(sizes)
    shapes = [jax.ShapeDtypeStruct((n, width), BF16) for n in sizes]
    if steps:
        shapes[0] = jax.ShapeDtypeStruct((sizes[0] + 16, width), BF16)
    return pl.pallas_call(
        functools.partial(difference_kernel, at, tuple(sizes), pieces),
        out_shape=tuple(shapes),
        in_specs=[HBM, HBM] + [VMEM] * len(steps),
        out_specs=(VMEM,) * len(sizes),
        scratch_shapes=[pltpu.VMEM((2, rows, width), F32), pltpu.SemaphoreType.DMA((2, pieces))],
        compiler_params=params(52),
        cost_estimate=cost(2 * rows * width, 10 * rows * width),
        name="difference",
    )(base, local, *steps)


def outer_kernel(base, mom, own, got, mine, theirs, *refs):
    new_base, new_mom = refs[-2:]
    mine = mine[...][0:1, :].astype(F32)
    theirs = theirs[...][0:1, :].astype(F32)
    scale = 1.0 / (mine + theirs)
    average = (mine * scale) * own[...].astype(F32) + (theirs * scale) * got[...].astype(F32)
    momentum = 0.9 * mom[...] + average
    new_mom[...] = momentum
    new_base[...] = base[...] - 0.7 * (average + 0.9 * momentum)


def outer(base, mom, own, got, mine, theirs, at, rows, block, state):
    width = own.shape[1]
    big = pl.BlockSpec((pl.Element(block), pl.Element(width)), lambda i: (pl.multiple_of(at + i * block, 16), 0))
    small = pl.BlockSpec((block, width), lambda i: (i, 0))
    counts = mine.shape[0] // 16 - 1
    steps = pl.BlockSpec((16, width), lambda i: (counts, 0))
    shape = jax.ShapeDtypeStruct(base.shape, F32)
    return pl.pallas_call(
        outer_kernel,
        out_shape=(shape, shape),
        grid=(rows // block,),
        in_specs=[big, big, small, small, steps, steps] + [ANY] * len(state),
        out_specs=(big, big),
        input_output_aliases={6 + i: i for i in range(len(state))},
        compiler_params=params(),
        cost_estimate=cost(10 * rows * width, 20 * rows * width),
        name="outer_step",
    )(base, mom, own, got, mine, theirs, *state)


def dot(a, b):
    return jnp.dot(a, b, preferred_element_type=F32)


def column(back, mine, depth):
    f = lax.axis_index("fsdp")
    z, y, c = f // 4, (f // 2) % 2, f % 2
    p = (z + y * (7 - 2 * z) - back * (1 - 2 * c) + 8) % 8
    far = p // 4
    z, y = p + far * (7 - 2 * p), far
    c = c if mine else 1 - c
    return pl.multiple_of(index(z, y, c) * depth, depth)


def partial_kernel(blocks, first, act, sib, *refs):
    refs, (own_out, sib_out) = refs[:-2], refs[-2:]
    weights, state = (refs, None) if first else (refs[:-2], refs[-2:])
    depth = act.shape[1] // 16
    own = None if first else state[0][...]
    theirs = None if first else state[1][...]
    for (back, mine), ref in zip(blocks, weights):
        w = ref[...]
        columns = pl.ds(column(back, mine, depth), depth)
        a, b = dot(act[:, columns], w), dot(sib[:, columns], w)
        own = a if own is None else own + a
        theirs = b if theirs is None else theirs + b
    own_out[...] = own
    sib_out[...] = theirs.astype(sib_out.dtype)


def partial_sums(blocks, act, sib, weights, state, kind=F32):
    tokens = act.shape[0]
    width = weights[0].shape[1]
    out = jax.ShapeDtypeStruct((tokens, width), F32)
    return pl.pallas_call(
        functools.partial(partial_kernel, blocks, not state),
        out_shape=(out, jax.ShapeDtypeStruct((tokens, width), kind)),
        in_specs=[VMEM] * (2 + len(weights) + len(state)),
        out_specs=(VMEM, VMEM),
        compiler_params=params(),
        cost_estimate=cost(0, 0),
        name="partial_keys",
    )(act, sib, *weights, *state)


def close_kernel(at, act, mine, other, own, got, base, mom, diff, sent, steps0, steps1, *refs):
    keys, new_base, new_mom, loaded, stored, done, sems = refs[-7:]
    rows = diff.shape[0]
    part = pl.ds(at, rows)
    loads = [
        pltpu.make_async_copy(ref.at[part, :], loaded.at[i], sems.at[i]) for i, ref in enumerate((base, mom))
    ]
    for copy in loads:
        copy.start()
    depth = mine.shape[0]
    total = own[...] + got[...].astype(F32)
    total += dot(act[:, pl.ds(column(4, True, depth), depth)], mine[...])
    total += dot(act[:, pl.ds(column(4, False, depth), depth)], other[...])
    done[...] = total.astype(BF16)
    stores = [pltpu.make_async_copy(done, keys, sems.at[2])]
    stores[0].start()
    n = steps0.shape[0]
    ours = steps0[pl.ds(n - 16, 16), :][0:1, :].astype(F32)
    theirs = steps1[pl.ds(n - 16, 16), :][0:1, :].astype(F32)
    scale = 1.0 / (ours + theirs)
    average = (ours * scale) * diff[...].astype(F32) + (theirs * scale) * sent[...].astype(F32)
    for copy in loads:
        copy.wait()
    momentum = 0.9 * loaded[1] + average
    stored[1] = momentum
    stored[0] = loaded[0] - 0.7 * (average + 0.9 * momentum)
    for i, ref in enumerate((new_base, new_mom)):
        stores.append(pltpu.make_async_copy(stored.at[i], ref.at[part, :], sems.at[3 + i]))
        stores[-1].start()
    for copy in stores:
        copy.wait()


def close(act, mine, other, own, got, base, mom, diff, sent, steps0, steps1, at, state):
    tokens, width = own.shape
    rows = diff.shape[0]
    shape = jax.ShapeDtypeStruct(base.shape, F32)
    return pl.pallas_call(
        functools.partial(close_kernel, at),
        out_shape=(jax.ShapeDtypeStruct((tokens, width), BF16), shape, shape),
        in_specs=[VMEM] * 5 + [ANY] * 2 + [VMEM] * 4 + [ANY] * 2,
        out_specs=(ANY, ANY, ANY),
        input_output_aliases={11: 1, 12: 2},
        scratch_shapes=[
            pltpu.VMEM((2, rows, width), F32),
            pltpu.VMEM((2, rows, width), F32),
            pltpu.VMEM((tokens, width), BF16),
            pltpu.SemaphoreType.DMA((5,)),
        ],
        compiler_params=params(),
        cost_estimate=cost(0, 0),
        name="close",
    )(act, mine, other, own, got, base, mom, diff, sent, steps0, steps1, *state)


def special(activations, inner_weight, local_params, base_params, momentum, inner_steps):
    shape = base_params.shape
    flat = lambda a: a.reshape(-1, shape[-1])
    base, mom, local = flat(base_params), flat(momentum), flat(local_params)
    w = inner_weight[0]

    rows = base.shape[0]
    n1 = rows * 4 // 16
    n0 = rows - n1
    sib = send_core(activations)
    own0, own1 = difference(base, local, 0, (n0, n1), 4, (inner_steps.reshape(1, 1),))
    got0, got1 = send_x(own0), send_x(own1)
    a1 = cycle(w)
    wsib = send_core(w)
    b1 = cycle(tie(wsib, sib, own0)[0])
    a2 = cycle(a1)
    b2 = cycle(b1)
    state = partial_sums(((0, True), (1, True), (1, False)), activations, sib, (w, a1, b1), ())
    a2, *state = tie(a2, *state)
    a3 = cycle(a2)
    b3 = cycle(b2)
    state = partial_sums(((2, True), (2, False)), activations, sib, (a2, b2), state)
    a3, *state = tie(a3, *state)
    last = cycle(a3)
    own_sum, sib_sum = partial_sums(((3, True), (3, False)), activations, sib, (a3, b3), state, BF16)
    swapped = send_core(sib_sum)
    got0, own_sum = tie(got0, own_sum)
    new = outer(base, mom, own0, got0, own0, got0, 0, n0, n0 // 2, ())
    last, *new = tie(last, *new)
    other = send_core(last)
    keys, *new = close(
        activations, last, other, own_sum, swapped, base, mom, own1, got1, own0, got0, n0, new
    )
    return (keys, new[0].reshape(shape), new[1].reshape(shape))


def solution(mesh):
    fast = mesh.shape["replica"] == 2 and mesh.shape["fsdp"] == 16
    return jax.shard_map(
        special if fast else general,
        mesh=mesh,
        in_specs=(
            P(("replica", "fsdp"), None),
            P("replica", "fsdp", None),
            P("replica", None, None, "fsdp", None),
            P(None, None, "fsdp", None),
            P(None, None, "fsdp", None),
            P("replica"),
        ),
        out_specs=(
            P(("replica", "fsdp"), None),
            P(None, None, "fsdp", None),
            P(None, None, "fsdp", None),
        ),
        check_vma=False,
    )
```

```python
import functools

import jax
import jax.numpy as jnp
from jax import lax
from jax.experimental import pallas as pl
from jax.experimental.pallas import tpu as pltpu
from jax.sharding import PartitionSpec as P

F32, BF16 = jnp.float32, jnp.bfloat16
MIB = 1024 * 1024
HBM = pl.BlockSpec(memory_space=pltpu.HBM)
ANY = pl.BlockSpec(memory_space=pl.ANY)
VMEM = pl.BlockSpec(memory_space=pltpu.VMEM)


def nesterov(average, momentum, base_params):
    new_momentum = 0.9 * momentum + average
    new_base = base_params - 0.7 * (average + 0.9 * new_momentum)
    return (new_base, new_momentum)


def general(activations, inner_weight, local_params, base_params, momentum, inner_steps):
    counts = lax.all_gather(inner_steps, "replica", axis=0, tiled=True)
    total = jnp.sum(counts.astype(F32))
    own = inner_steps[0].astype(F32)
    difference = (base_params - local_params[0]).astype(BF16)
    average = lax.psum(own * difference.astype(F32), "replica") / total
    new_base, new_momentum = nesterov(average, momentum, base_params)
    weight = lax.all_gather(inner_weight[0], "fsdp", axis=0, tiled=True)
    keys = jnp.dot(activations, weight, preferred_element_type=F32).astype(BF16)
    return (keys, new_base, new_momentum)


def index(z, y, c):
    return (z * 2 + y) * 2 + c


def place(p):
    p = p % 8
    return (p, 0) if p < 4 else (7 - p, 1)


def cycle(x):
    pairs = [
        (index(*place(p), c), index(*place(p + 1 - 2 * c), c)) for p in range(8) for c in range(2)
    ]
    return lax.ppermute(x, "fsdp", pairs)


def send_core(x):
    pairs = [(i, i ^ 1) for i in range(16)]
    return lax.ppermute(x, "fsdp", pairs)


def send_x(x):
    return lax.ppermute(x, "replica", [(0, 1), (1, 0)])


def tie(*xs):
    return lax.optimization_barrier(xs)


def cost(flops, bytes_accessed):
    return pl.CostEstimate(flops=int(flops), bytes_accessed=int(bytes_accessed), transcendentals=0)


def params(limit=16):
    return pltpu.CompilerParams(vmem_limit_bytes=limit * MIB)


def difference_kernel(at, sizes, pieces, base, local, *refs):
    held, sems = refs[-2:]
    outs = refs[-2 - len(sizes):-2]
    rows = held.shape[1]
    piece = rows // pieces
    copies = []
    for j in range(pieces):
        for i, ref in enumerate((base, local)):
            part = pl.ds(j * piece, piece)
            copies.append(
                pltpu.make_async_copy(ref.at[pl.ds(at + j * piece, piece), :], held.at[i, part, :], sems.at[i, j])
            )
    for copy in copies:
        copy.start()
    extra = outs[0].shape[0] - sizes[0]
    if extra:
        count = jnp.broadcast_to(refs[0][...].astype(F32), (extra, outs[0].shape[1]))
        outs[0][pl.ds(sizes[0], extra), :] = count.astype(BF16)
    which, put = 0, 0
    for j in range(pieces):
        copies[2 * j].wait()
        copies[2 * j + 1].wait()
        part = pl.ds(j * piece, piece)
        outs[which][pl.ds(put, piece), :] = (held[0, part, :] - held[1, part, :]).astype(BF16)
        put += piece
        if put == sizes[which]:
            which, put = which + 1, 0


def difference(base, local, at, sizes, pieces, steps=()):
    width = base.shape[1]
    rows = sum(sizes)
    shapes = [jax.ShapeDtypeStruct((n, width), BF16) for n in sizes]
    if steps:
        shapes[0] = jax.ShapeDtypeStruct((sizes[0] + 16, width), BF16)
    return pl.pallas_call(
        functools.partial(difference_kernel, at, tuple(sizes), pieces),
        out_shape=tuple(shapes),
        in_specs=[HBM, HBM] + [VMEM] * len(steps),
        out_specs=(VMEM,) * len(sizes),
        scratch_shapes=[pltpu.VMEM((2, rows, width), F32), pltpu.SemaphoreType.DMA((2, pieces))],
        compiler_params=params(52 if at == 0 else 16),
        cost_estimate=cost(2 * rows * width, 10 * rows * width),
        name="difference",
    )(base, local, *steps)


def outer_kernel(base, mom, own, got, mine, theirs, *refs):
    new_base, new_mom = refs[-2:]
    mine = mine[...][0:1, :].astype(F32)
    theirs = theirs[...][0:1, :].astype(F32)
    scale = 1.0 / (mine + theirs)
    average = (mine * scale) * own[...].astype(F32) + (theirs * scale) * got[...].astype(F32)
    momentum = 0.9 * mom[...] + average
    new_mom[...] = momentum
    new_base[...] = base[...] - 0.7 * (average + 0.9 * momentum)


def outer(base, mom, own, got, mine, theirs, at, rows, block, state):
    width = own.shape[1]
    big = pl.BlockSpec((pl.Element(block), pl.Element(width)), lambda i: (pl.multiple_of(at + i * block, 16), 0))
    small = pl.BlockSpec((block, width), lambda i: (i, 0))
    counts = mine.shape[0] // 16 - 1
    steps = pl.BlockSpec((16, width), lambda i: (counts, 0))
    shape = jax.ShapeDtypeStruct(base.shape, F32)
    return pl.pallas_call(
        outer_kernel,
        out_shape=(shape, shape),
        grid=(rows // block,),
        in_specs=[big, big, small, small, steps, steps] + [ANY] * len(state),
        out_specs=(big, big),
        input_output_aliases={6 + i: i for i in range(len(state))},
        compiler_params=params(),
        cost_estimate=cost(10 * rows * width, 20 * rows * width),
        name="outer_step",
    )(base, mom, own, got, mine, theirs, *state)


def dot(a, b):
    return jnp.dot(a, b, preferred_element_type=F32)


def column(back, mine, depth):
    f = lax.axis_index("fsdp")
    z, y, c = f // 4, (f // 2) % 2, f % 2
    p = (z + y * (7 - 2 * z) - back * (1 - 2 * c) + 8) % 8
    far = p // 4
    z, y = p + far * (7 - 2 * p), far
    c = c if mine else 1 - c
    return pl.multiple_of(index(z, y, c) * depth, depth)


def partial_kernel(blocks, first, act, sib, *refs):
    refs, (own_out, sib_out) = refs[:-2], refs[-2:]
    weights, state = (refs, None) if first else (refs[:-2], refs[-2:])
    depth = act.shape[1] // 16
    own = None if first else state[0][...]
    theirs = None if first else state[1][...]
    for (back, mine), ref in zip(blocks, weights):
        w = ref[...]
        columns = pl.ds(column(back, mine, depth), depth)
        a, b = dot(act[:, columns], w), dot(sib[:, columns], w)
        own = a if own is None else own + a
        theirs = b if theirs is None else theirs + b
    own_out[...] = own
    sib_out[...] = theirs.astype(sib_out.dtype)


def partial_sums(blocks, act, sib, weights, state, kind=F32):
    tokens = act.shape[0]
    width = weights[0].shape[1]
    out = jax.ShapeDtypeStruct((tokens, width), F32)
    return pl.pallas_call(
        functools.partial(partial_kernel, blocks, not state),
        out_shape=(out, jax.ShapeDtypeStruct((tokens, width), kind)),
        in_specs=[VMEM] * (2 + len(weights) + len(state)),
        out_specs=(VMEM, VMEM),
        compiler_params=params(),
        cost_estimate=cost(0, 0),
        name="partial_keys",
    )(act, sib, *weights, *state)


def close_kernel(at, act, mine, other, own, got, base, mom, diff, sent, steps0, steps1, *refs):
    keys, new_base, new_mom, loaded, stored, done, sems = refs[-7:]
    rows = diff.shape[0]
    part = pl.ds(at, rows)
    loads = [
        pltpu.make_async_copy(ref.at[part, :], loaded.at[i], sems.at[i]) for i, ref in enumerate((base, mom))
    ]
    for copy in loads:
        copy.start()
    depth = mine.shape[0]
    total = own[...] + got[...].astype(F32)
    total += dot(act[:, pl.ds(column(4, True, depth), depth)], mine[...])
    total += dot(act[:, pl.ds(column(4, False, depth), depth)], other[...])
    done[...] = total.astype(BF16)
    stores = [pltpu.make_async_copy(done, keys, sems.at[2])]
    stores[0].start()
    n = steps0.shape[0]
    ours = steps0[pl.ds(n - 16, 16), :][0:1, :].astype(F32)
    theirs = steps1[pl.ds(n - 16, 16), :][0:1, :].astype(F32)
    scale = 1.0 / (ours + theirs)
    average = (ours * scale) * diff[...].astype(F32) + (theirs * scale) * sent[...].astype(F32)
    for copy in loads:
        copy.wait()
    momentum = 0.9 * loaded[1] + average
    stored[1] = momentum
    stored[0] = loaded[0] - 0.7 * (average + 0.9 * momentum)
    for i, ref in enumerate((new_base, new_mom)):
        stores.append(pltpu.make_async_copy(stored.at[i], ref.at[part, :], sems.at[3 + i]))
        stores[-1].start()
    for copy in stores:
        copy.wait()


def close(act, mine, other, own, got, base, mom, diff, sent, steps0, steps1, at, state):
    tokens, width = own.shape
    rows = diff.shape[0]
    shape = jax.ShapeDtypeStruct(base.shape, F32)
    return pl.pallas_call(
        functools.partial(close_kernel, at),
        out_shape=(jax.ShapeDtypeStruct((tokens, width), BF16), shape, shape),
        in_specs=[VMEM] * 5 + [ANY] * 2 + [VMEM] * 4 + [ANY] * 2,
        out_specs=(ANY, ANY, ANY),
        input_output_aliases={11: 1, 12: 2},
        scratch_shapes=[
            pltpu.VMEM((2, rows, width), F32),
            pltpu.VMEM((2, rows, width), F32),
            pltpu.VMEM((tokens, width), BF16),
            pltpu.SemaphoreType.DMA((5,)),
        ],
        compiler_params=params(),
        cost_estimate=cost(0, 0),
        name="close",
    )(act, mine, other, own, got, base, mom, diff, sent, steps0, steps1, *state)


def special(activations, inner_weight, local_params, base_params, momentum, inner_steps):
    shape = base_params.shape
    flat = lambda a: a.reshape(-1, shape[-1])
    base, mom, local = flat(base_params), flat(momentum), flat(local_params)
    w = inner_weight[0]

    rows = base.shape[0]
    n1 = rows * 4 // 16
    n0 = rows - n1
    sib = send_core(activations)
    (own0,) = difference(base, local, 0, (n0,), 3, (inner_steps.reshape(1, 1),))
    (own1,) = difference(tie(base, own0)[0], local, n0, (n1,), 1)
    got0 = send_x(own0)
    a1 = cycle(w)
    wsib = send_core(w)
    b1 = cycle(tie(wsib, sib, own0)[0])
    a2 = cycle(a1)
    b1, own1 = tie(b1, own1)
    got1 = send_x(own1)
    b2 = cycle(b1)
    state = partial_sums(((0, True), (1, True), (1, False)), activations, sib, (w, a1, b1), ())
    a2, *state = tie(a2, *state)
    a3 = cycle(a2)
    b3 = cycle(b2)
    state = partial_sums(((2, True), (2, False)), activations, sib, (a2, b2), state)
    a3, *state = tie(a3, *state)
    last = cycle(a3)
    own_sum, sib_sum = partial_sums(((3, True), (3, False)), activations, sib, (a3, b3), state, BF16)
    swapped = send_core(sib_sum)
    got0, own_sum = tie(got0, own_sum)
    new = outer(base, mom, own0, got0, own0, got0, 0, n0, n0 // 2, ())
    last, *new = tie(last, *new)
    other = send_core(last)
    keys, *new = close(
        activations, last, other, own_sum, swapped, base, mom, own1, got1, own0, got0, n0, new
    )
    return (keys, new[0].reshape(shape), new[1].reshape(shape))


def solution(mesh):
    fast = mesh.shape["replica"] == 2 and mesh.shape["fsdp"] == 16
    return jax.shard_map(
        special if fast else general,
        mesh=mesh,
        in_specs=(
            P(("replica", "fsdp"), None),
            P("replica", "fsdp", None),
            P("replica", None, None, "fsdp", None),
            P(None, None, "fsdp", None),
            P(None, None, "fsdp", None),
            P("replica"),
        ),
        out_specs=(
            P(("replica", "fsdp"), None),
            P(None, None, "fsdp", None),
            P(None, None, "fsdp", None),
        ),
        check_vma=False,
    )
```

```python
import functools

import jax
import jax.numpy as jnp
from jax import lax
from jax.experimental import pallas as pl
from jax.experimental.pallas import tpu as pltpu
from jax.sharding import PartitionSpec as P

F32, BF16 = jnp.float32, jnp.bfloat16
MIB = 1024 * 1024
HBM = pl.BlockSpec(memory_space=pltpu.HBM)
ANY = pl.BlockSpec(memory_space=pl.ANY)
VMEM = pl.BlockSpec(memory_space=pltpu.VMEM)


def nesterov(average, momentum, base_params):
    new_momentum = 0.9 * momentum + average
    new_base = base_params - 0.7 * (average + 0.9 * new_momentum)
    return (new_base, new_momentum)


def general(activations, inner_weight, local_params, base_params, momentum, inner_steps):
    counts = lax.all_gather(inner_steps, "replica", axis=0, tiled=True)
    total = jnp.sum(counts.astype(F32))
    own = inner_steps[0].astype(F32)
    difference = (base_params - local_params[0]).astype(BF16)
    average = lax.psum(own * difference.astype(F32), "replica") / total
    new_base, new_momentum = nesterov(average, momentum, base_params)
    weight = lax.all_gather(inner_weight[0], "fsdp", axis=0, tiled=True)
    keys = jnp.dot(activations, weight, preferred_element_type=F32).astype(BF16)
    return (keys, new_base, new_momentum)


def index(z, y, c):
    return (z * 2 + y) * 2 + c


def place(p):
    p = p % 8
    return (p, 0) if p < 4 else (7 - p, 1)


def cycle(x):
    pairs = [
        (index(*place(p), c), index(*place(p + 1 - 2 * c), c)) for p in range(8) for c in range(2)
    ]
    return lax.ppermute(x, "fsdp", pairs)


def send_core(x):
    pairs = [(i, i ^ 1) for i in range(16)]
    return lax.ppermute(x, "fsdp", pairs)


def send_x(x):
    return lax.ppermute(x, "replica", [(0, 1), (1, 0)])


def tie(*xs):
    return lax.optimization_barrier(xs)


def cost(flops, bytes_accessed):
    return pl.CostEstimate(flops=int(flops), bytes_accessed=int(bytes_accessed), transcendentals=0)


def params(limit=16):
    return pltpu.CompilerParams(vmem_limit_bytes=limit * MIB)


def difference_kernel(at, sizes, pieces, base, local, *refs):
    held, sems = refs[-2:]
    outs = refs[-2 - len(sizes):-2]
    rows = held.shape[1]
    piece = rows // pieces
    copies = []
    for j in range(pieces):
        for i, ref in enumerate((base, local)):
            part = pl.ds(j * piece, piece)
            copies.append(
                pltpu.make_async_copy(ref.at[pl.ds(at + j * piece, piece), :], held.at[i, part, :], sems.at[i, j])
            )
    for copy in copies:
        copy.start()
    extra = outs[0].shape[0] - sizes[0]
    if extra:
        count = jnp.broadcast_to(refs[0][...].astype(F32), (extra, outs[0].shape[1]))
        outs[0][pl.ds(sizes[0], extra), :] = count.astype(BF16)
    which, put = 0, 0
    for j in range(pieces):
        copies[2 * j].wait()
        copies[2 * j + 1].wait()
        part = pl.ds(j * piece, piece)
        outs[which][pl.ds(put, piece), :] = (held[0, part, :] - held[1, part, :]).astype(BF16)
        put += piece
        if put == sizes[which]:
            which, put = which + 1, 0


def difference(base, local, at, sizes, pieces, steps=()):
    width = base.shape[1]
    rows = sum(sizes)
    shapes = [jax.ShapeDtypeStruct((n, width), BF16) for n in sizes]
    if steps:
        shapes[0] = jax.ShapeDtypeStruct((sizes[0] + 16, width), BF16)
    return pl.pallas_call(
        functools.partial(difference_kernel, at, tuple(sizes), pieces),
        out_shape=tuple(shapes),
        in_specs=[HBM, HBM] + [VMEM] * len(steps),
        out_specs=(VMEM,) * len(sizes),
        scratch_shapes=[pltpu.VMEM((2, rows, width), F32), pltpu.SemaphoreType.DMA((2, pieces))],
        compiler_params=params(52 if at == 0 else 16),
        cost_estimate=cost(2 * rows * width, 10 * rows * width),
        name="difference",
    )(base, local, *steps)


def outer_kernel(base, mom, own, got, mine, theirs, *refs):
    new_base, new_mom = refs[-2:]
    mine = mine[...][0:1, :].astype(F32)
    theirs = theirs[...][0:1, :].astype(F32)
    scale = 1.0 / (mine + theirs)
    average = (mine * scale) * own[...].astype(F32) + (theirs * scale) * got[...].astype(F32)
    momentum = 0.9 * mom[...] + average
    new_mom[...] = momentum
    new_base[...] = base[...] - 0.7 * (average + 0.9 * momentum)


def outer(base, mom, own, got, mine, theirs, at, rows, block, state):
    width = own.shape[1]
    big = pl.BlockSpec((pl.Element(block), pl.Element(width)), lambda i: (pl.multiple_of(at + i * block, 16), 0))
    small = pl.BlockSpec((block, width), lambda i: (i, 0))
    counts = mine.shape[0] // 16 - 1
    steps = pl.BlockSpec((16, width), lambda i: (counts, 0))
    shape = jax.ShapeDtypeStruct(base.shape, F32)
    return pl.pallas_call(
        outer_kernel,
        out_shape=(shape, shape),
        grid=(rows // block,),
        in_specs=[big, big, small, small, steps, steps] + [ANY] * len(state),
        out_specs=(big, big),
        input_output_aliases={6 + i: i for i in range(len(state))},
        compiler_params=params(),
        cost_estimate=cost(10 * rows * width, 20 * rows * width),
        name="outer_step",
    )(base, mom, own, got, mine, theirs, *state)


def dot(a, b):
    return jnp.dot(a, b, preferred_element_type=F32)


def column(back, mine, depth):
    f = lax.axis_index("fsdp")
    z, y, c = f // 4, (f // 2) % 2, f % 2
    p = (z + y * (7 - 2 * z) - back * (1 - 2 * c) + 8) % 8
    far = p // 4
    z, y = p + far * (7 - 2 * p), far
    c = c if mine else 1 - c
    return pl.multiple_of(index(z, y, c) * depth, depth)


def partial_kernel(blocks, first, act, sib, *refs):
    refs, (own_out, sib_out) = refs[:-2], refs[-2:]
    weights, state = (refs, None) if first else (refs[:-2], refs[-2:])
    depth = act.shape[1] // 16
    own = None if first else state[0][...]
    theirs = None if first else state[1][...]
    for (back, mine), ref in zip(blocks, weights):
        w = ref[...]
        columns = pl.ds(column(back, mine, depth), depth)
        a, b = dot(act[:, columns], w), dot(sib[:, columns], w)
        own = a if own is None else own + a
        theirs = b if theirs is None else theirs + b
    own_out[...] = own
    sib_out[...] = theirs.astype(sib_out.dtype)


def partial_sums(blocks, act, sib, weights, state, kind=F32):
    tokens = act.shape[0]
    width = weights[0].shape[1]
    out = jax.ShapeDtypeStruct((tokens, width), F32)
    return pl.pallas_call(
        functools.partial(partial_kernel, blocks, not state),
        out_shape=(out, jax.ShapeDtypeStruct((tokens, width), kind)),
        in_specs=[VMEM] * (2 + len(weights) + len(state)),
        out_specs=(VMEM, VMEM),
        compiler_params=params(),
        cost_estimate=cost(0, 0),
        name="partial_keys",
    )(act, sib, *weights, *state)


def close_kernel(at, act, mine, other, own, got, base, mom, diff, sent, steps0, steps1, *refs):
    keys, new_base, new_mom, loaded, stored, done, sems = refs[-7:]
    rows = diff.shape[0]
    part = pl.ds(at, rows)
    loads = [
        pltpu.make_async_copy(ref.at[part, :], loaded.at[i], sems.at[i]) for i, ref in enumerate((base, mom))
    ]
    for copy in loads:
        copy.start()
    depth = mine.shape[0]
    total = own[...] + got[...].astype(F32)
    total += dot(act[:, pl.ds(column(4, True, depth), depth)], mine[...])
    total += dot(act[:, pl.ds(column(4, False, depth), depth)], other[...])
    done[...] = total.astype(BF16)
    stores = [pltpu.make_async_copy(done, keys, sems.at[2])]
    stores[0].start()
    n = steps0.shape[0]
    ours = steps0[pl.ds(n - 16, 16), :][0:1, :].astype(F32)
    theirs = steps1[pl.ds(n - 16, 16), :][0:1, :].astype(F32)
    scale = 1.0 / (ours + theirs)
    average = (ours * scale) * diff[...].astype(F32) + (theirs * scale) * sent[...].astype(F32)
    for copy in loads:
        copy.wait()
    half = rows // 2
    for j in range(2):
        cut = slice(j * half, (j + 1) * half)
        here, there = pl.ds(j * half, half), pl.ds(at + j * half, half)
        momentum = 0.9 * loaded[1, here, :] + average[cut]
        stored[1, here, :] = momentum
        stored[0, here, :] = loaded[0, here, :] - 0.7 * (average[cut] + 0.9 * momentum)
        for i, ref in enumerate((new_base, new_mom)):
            stores.append(
                pltpu.make_async_copy(stored.at[i, here, :], ref.at[there, :], sems.at[3 + 2 * j + i])
            )
            stores[-1].start()
    for copy in stores:
        copy.wait()


def close(act, mine, other, own, got, base, mom, diff, sent, steps0, steps1, at, state):
    tokens, width = own.shape
    rows = diff.shape[0]
    shape = jax.ShapeDtypeStruct(base.shape, F32)
    return pl.pallas_call(
        functools.partial(close_kernel, at),
        out_shape=(jax.ShapeDtypeStruct((tokens, width), BF16), shape, shape),
        in_specs=[VMEM] * 5 + [ANY] * 2 + [VMEM] * 4 + [ANY] * 2,
        out_specs=(ANY, ANY, ANY),
        input_output_aliases={11: 1, 12: 2},
        scratch_shapes=[
            pltpu.VMEM((2, rows, width), F32),
            pltpu.VMEM((2, rows, width), F32),
            pltpu.VMEM((tokens, width), BF16),
            pltpu.SemaphoreType.DMA((7,)),
        ],
        compiler_params=params(),
        cost_estimate=cost(0, 0),
        name="close",
    )(act, mine, other, own, got, base, mom, diff, sent, steps0, steps1, *state)


def special(activations, inner_weight, local_params, base_params, momentum, inner_steps):
    shape = base_params.shape
    flat = lambda a: a.reshape(-1, shape[-1])
    base, mom, local = flat(base_params), flat(momentum), flat(local_params)
    w = inner_weight[0]

    rows = base.shape[0]
    n1 = rows * 4 // 16
    n0 = rows - n1
    sib = send_core(activations)
    (own0,) = difference(base, local, 0, (n0,), 6, (inner_steps.reshape(1, 1),))
    (own1,) = difference(tie(base, own0)[0], local, n0, (n1,), 1)
    got0 = send_x(own0)
    a1 = cycle(w)
    wsib = send_core(w)
    b1 = cycle(tie(wsib, own0)[0])
    a2 = cycle(a1)
    b1, own1 = tie(b1, own1)
    got1 = send_x(own1)
    b2 = cycle(b1)
    state = partial_sums(((0, True), (1, True), (1, False)), activations, sib, (w, a1, b1), ())
    a2, *state = tie(a2, *state)
    a3 = cycle(a2)
    b3 = cycle(b2)
    state = partial_sums(((2, True), (2, False)), activations, sib, (a2, b2), state)
    a3, *state = tie(a3, *state)
    last = cycle(a3)
    own_sum, sib_sum = partial_sums(((3, True), (3, False)), activations, sib, (a3, b3), state, BF16)
    swapped = send_core(sib_sum)
    got0, own_sum = tie(got0, own_sum)
    new = outer(base, mom, own0, got0, own0, got0, 0, n0, n0 // 2, ())
    last, *new = tie(last, *new)
    other = send_core(last)
    keys, *new = close(
        activations, last, other, own_sum, swapped, base, mom, own1, got1, own0, got0, n0, new
    )
    return (keys, new[0].reshape(shape), new[1].reshape(shape))


def solution(mesh):
    fast = mesh.shape["replica"] == 2 and mesh.shape["fsdp"] == 16
    return jax.shard_map(
        special if fast else general,
        mesh=mesh,
        in_specs=(
            P(("replica", "fsdp"), None),
            P("replica", "fsdp", None),
            P("replica", None, None, "fsdp", None),
            P(None, None, "fsdp", None),
            P(None, None, "fsdp", None),
            P("replica"),
        ),
        out_specs=(
            P(("replica", "fsdp"), None),
            P(None, None, "fsdp", None),
            P(None, None, "fsdp", None),
        ),
        check_vma=False,
    )
```

```python
import functools

import jax
import jax.numpy as jnp
from jax import lax
from jax.experimental import pallas as pl
from jax.experimental.pallas import tpu as pltpu
from jax.sharding import PartitionSpec as P

F32, BF16 = jnp.float32, jnp.bfloat16
MIB = 1024 * 1024
HBM = pl.BlockSpec(memory_space=pltpu.HBM)
ANY = pl.BlockSpec(memory_space=pl.ANY)
VMEM = pl.BlockSpec(memory_space=pltpu.VMEM)


def nesterov(average, momentum, base_params):
    new_momentum = 0.9 * momentum + average
    new_base = base_params - 0.7 * (average + 0.9 * new_momentum)
    return (new_base, new_momentum)


def general(activations, inner_weight, local_params, base_params, momentum, inner_steps):
    counts = lax.all_gather(inner_steps, "replica", axis=0, tiled=True)
    total = jnp.sum(counts.astype(F32))
    own = inner_steps[0].astype(F32)
    difference = (base_params - local_params[0]).astype(BF16)
    average = lax.psum(own * difference.astype(F32), "replica") / total
    new_base, new_momentum = nesterov(average, momentum, base_params)
    weight = lax.all_gather(inner_weight[0], "fsdp", axis=0, tiled=True)
    keys = jnp.dot(activations, weight, preferred_element_type=F32).astype(BF16)
    return (keys, new_base, new_momentum)


def index(z, y, c):
    return (z * 2 + y) * 2 + c


def place(p):
    p = p % 8
    return (p, 0) if p < 4 else (7 - p, 1)


def cycle(x):
    pairs = [
        (index(*place(p), c), index(*place(p + 1 - 2 * c), c)) for p in range(8) for c in range(2)
    ]
    return lax.ppermute(x, "fsdp", pairs)


def send_core(x):
    pairs = [(i, i ^ 1) for i in range(16)]
    return lax.ppermute(x, "fsdp", pairs)


def send_x(x):
    return lax.ppermute(x, "replica", [(0, 1), (1, 0)])


def tie(*xs):
    return lax.optimization_barrier(xs)


def cost(flops, bytes_accessed):
    return pl.CostEstimate(flops=int(flops), bytes_accessed=int(bytes_accessed), transcendentals=0)


def params(limit=16):
    return pltpu.CompilerParams(vmem_limit_bytes=limit * MIB)


def difference_kernel(at, sizes, pieces, base, local, *refs):
    held, sems = refs[-2:]
    outs = refs[-2 - len(sizes):-2]
    rows = held.shape[1]
    piece = rows // pieces
    copies = []
    for j in range(pieces):
        for i, ref in enumerate((base, local)):
            part = pl.ds(j * piece, piece)
            copies.append(
                pltpu.make_async_copy(ref.at[pl.ds(at + j * piece, piece), :], held.at[i, part, :], sems.at[i, j])
            )
    for copy in copies:
        copy.start()
    extra = outs[0].shape[0] - sizes[0]
    if extra:
        count = jnp.broadcast_to(refs[0][...].astype(F32), (extra, outs[0].shape[1]))
        outs[0][pl.ds(sizes[0], extra), :] = count.astype(BF16)
    which, put = 0, 0
    for j in range(pieces):
        copies[2 * j].wait()
        copies[2 * j + 1].wait()
        part = pl.ds(j * piece, piece)
        outs[which][pl.ds(put, piece), :] = (held[0, part, :] - held[1, part, :]).astype(BF16)
        put += piece
        if put == sizes[which]:
            which, put = which + 1, 0


def difference(base, local, at, sizes, pieces, steps=()):
    width = base.shape[1]
    rows = sum(sizes)
    shapes = [jax.ShapeDtypeStruct((n, width), BF16) for n in sizes]
    if steps:
        shapes[0] = jax.ShapeDtypeStruct((sizes[0] + 16, width), BF16)
    return pl.pallas_call(
        functools.partial(difference_kernel, at, tuple(sizes), pieces),
        out_shape=tuple(shapes),
        in_specs=[HBM, HBM] + [VMEM] * len(steps),
        out_specs=(VMEM,) * len(sizes),
        scratch_shapes=[pltpu.VMEM((2, rows, width), F32), pltpu.SemaphoreType.DMA((2, pieces))],
        compiler_params=params(52 if at == 0 else 16),
        cost_estimate=cost(2 * rows * width, 10 * rows * width),
        name="difference",
    )(base, local, *steps)


def outer_kernel(base, mom, own, got, mine, theirs, *refs):
    new_base, new_mom = refs[-2:]
    mine = mine[...][0:1, :].astype(F32)
    theirs = theirs[...][0:1, :].astype(F32)
    scale = 1.0 / (mine + theirs)
    average = (mine * scale) * own[...].astype(F32) + (theirs * scale) * got[...].astype(F32)
    momentum = 0.9 * mom[...] + average
    new_mom[...] = momentum
    new_base[...] = base[...] - 0.7 * (average + 0.9 * momentum)


def outer(base, mom, own, got, mine, theirs, at, rows, block, state):
    width = own.shape[1]
    big = pl.BlockSpec((pl.Element(block), pl.Element(width)), lambda i: (pl.multiple_of(at + i * block, 16), 0))
    small = pl.BlockSpec((block, width), lambda i: (i, 0))
    counts = mine.shape[0] // 16 - 1
    steps = pl.BlockSpec((16, width), lambda i: (counts, 0))
    shape = jax.ShapeDtypeStruct(base.shape, F32)
    return pl.pallas_call(
        outer_kernel,
        out_shape=(shape, shape),
        grid=(rows // block,),
        in_specs=[big, big, small, small, steps, steps] + [ANY] * len(state),
        out_specs=(big, big),
        input_output_aliases={6 + i: i for i in range(len(state))},
        compiler_params=params(),
        cost_estimate=cost(10 * rows * width, 20 * rows * width),
        name="outer_step",
    )(base, mom, own, got, mine, theirs, *state)


def dot(a, b):
    return jnp.dot(a, b, preferred_element_type=F32)


def column(back, mine, depth):
    f = lax.axis_index("fsdp")
    z, y, c = f // 4, (f // 2) % 2, f % 2
    p = (z + y * (7 - 2 * z) - back * (1 - 2 * c) + 8) % 8
    far = p // 4
    z, y = p + far * (7 - 2 * p), far
    c = c if mine else 1 - c
    return pl.multiple_of(index(z, y, c) * depth, depth)


def partial_kernel(blocks, first, act, sib, *refs):
    refs, (own_out, sib_out) = refs[:-2], refs[-2:]
    weights, state = (refs, None) if first else (refs[:-2], refs[-2:])
    depth = act.shape[1] // 16
    own = None if first else state[0][...]
    theirs = None if first else state[1][...]
    for (back, mine), ref in zip(blocks, weights):
        w = ref[...]
        columns = pl.ds(column(back, mine, depth), depth)
        a, b = dot(act[:, columns], w), dot(sib[:, columns], w)
        own = a if own is None else own + a
        theirs = b if theirs is None else theirs + b
    own_out[...] = own
    sib_out[...] = theirs.astype(sib_out.dtype)


def partial_sums(blocks, act, sib, weights, state, kind=F32):
    tokens = act.shape[0]
    width = weights[0].shape[1]
    out = jax.ShapeDtypeStruct((tokens, width), F32)
    return pl.pallas_call(
        functools.partial(partial_kernel, blocks, not state),
        out_shape=(out, jax.ShapeDtypeStruct((tokens, width), kind)),
        in_specs=[VMEM] * (2 + len(weights) + len(state)),
        out_specs=(VMEM, VMEM),
        compiler_params=params(),
        cost_estimate=cost(0, 0),
        name="partial_keys",
    )(act, sib, *weights, *state)


def close_kernel(at, act, mine, other, own, got, base, mom, diff, sent, steps0, steps1, *refs):
    keys, new_base, new_mom, loaded, stored, done, sems = refs[-7:]
    rows = diff.shape[0]
    part = pl.ds(at, rows)
    loads = [
        pltpu.make_async_copy(ref.at[part, :], loaded.at[i], sems.at[i]) for i, ref in enumerate((base, mom))
    ]
    for copy in loads:
        copy.start()
    depth = mine.shape[0]
    total = own[...] + got[...].astype(F32)
    total += dot(act[:, pl.ds(column(4, True, depth), depth)], mine[...])
    total += dot(act[:, pl.ds(column(4, False, depth), depth)], other[...])
    done[...] = total.astype(BF16)
    stores = [pltpu.make_async_copy(done, keys, sems.at[2])]
    stores[0].start()
    n = steps0.shape[0]
    ours = steps0[pl.ds(n - 16, 16), :][0:1, :].astype(F32)
    theirs = steps1[pl.ds(n - 16, 16), :][0:1, :].astype(F32)
    scale = 1.0 / (ours + theirs)
    average = (ours * scale) * diff[...].astype(F32) + (theirs * scale) * sent[...].astype(F32)
    for copy in loads:
        copy.wait()
    half = rows // 2
    for j in range(2):
        cut = slice(j * half, (j + 1) * half)
        here, there = pl.ds(j * half, half), pl.ds(at + j * half, half)
        momentum = 0.9 * loaded[1, here, :] + average[cut]
        stored[1, here, :] = momentum
        stored[0, here, :] = loaded[0, here, :] - 0.7 * (average[cut] + 0.9 * momentum)
        for i, ref in enumerate((new_base, new_mom)):
            stores.append(
                pltpu.make_async_copy(stored.at[i, here, :], ref.at[there, :], sems.at[3 + 2 * j + i])
            )
            stores[-1].start()
    for copy in stores:
        copy.wait()


def close(act, mine, other, own, got, base, mom, diff, sent, steps0, steps1, at, state):
    tokens, width = own.shape
    rows = diff.shape[0]
    shape = jax.ShapeDtypeStruct(base.shape, F32)
    return pl.pallas_call(
        functools.partial(close_kernel, at),
        out_shape=(jax.ShapeDtypeStruct((tokens, width), BF16), shape, shape),
        in_specs=[VMEM] * 5 + [ANY] * 2 + [VMEM] * 4 + [ANY] * 2,
        out_specs=(ANY, ANY, ANY),
        input_output_aliases={11: 1, 12: 2},
        scratch_shapes=[
            pltpu.VMEM((2, rows, width), F32),
            pltpu.VMEM((2, rows, width), F32),
            pltpu.VMEM((tokens, width), BF16),
            pltpu.SemaphoreType.DMA((7,)),
        ],
        compiler_params=params(),
        cost_estimate=cost(0, 0),
        name="close",
    )(act, mine, other, own, got, base, mom, diff, sent, steps0, steps1, *state)


def special(activations, inner_weight, local_params, base_params, momentum, inner_steps):
    shape = base_params.shape
    flat = lambda a: a.reshape(-1, shape[-1])
    base, mom, local = flat(base_params), flat(momentum), flat(local_params)
    w = inner_weight[0]

    rows = base.shape[0]
    n1 = rows * 4 // 16
    n0 = rows - n1
    sib = send_core(activations)
    (own0,) = difference(base, local, 0, (n0,), 6, (inner_steps.reshape(1, 1),))
    (own1,) = difference(tie(base, own0)[0], local, n0, (n1,), 1)
    got0 = send_x(own0)
    a1 = cycle(w)
    wsib = send_core(w)
    b1 = cycle(tie(wsib, own0)[0])
    a2 = cycle(a1)
    b1, own1 = tie(b1, own1)
    got1 = send_x(own1)
    b2 = cycle(b1)
    state = partial_sums(((0, True), (1, True), (1, False)), activations, sib, (w, a1, b1), ())
    a2, *state = tie(a2, *state)
    a3 = cycle(a2)
    b3 = cycle(b2)
    state = partial_sums(((2, True), (2, False)), activations, sib, (a2, b2), state)
    a3, *state = tie(a3, *state)
    last = cycle(a3)
    own_sum, sib_sum = partial_sums(((3, True), (3, False)), activations, sib, (a3, b3), state, BF16)
    swapped = send_core(sib_sum)
    got0, own_sum = tie(got0, own_sum)
    new = outer(base, mom, own0, got0, own0, got0, 0, n0, n0 // 3, ())
    last, *new = tie(last, *new)
    other = send_core(last)
    keys, *new = close(
        activations, last, other, own_sum, swapped, base, mom, own1, got1, own0, got0, n0, new
    )
    return (keys, new[0].reshape(shape), new[1].reshape(shape))


def solution(mesh):
    fast = mesh.shape["replica"] == 2 and mesh.shape["fsdp"] == 16
    return jax.shard_map(
        special if fast else general,
        mesh=mesh,
        in_specs=(
            P(("replica", "fsdp"), None),
            P("replica", "fsdp", None),
            P("replica", None, None, "fsdp", None),
            P(None, None, "fsdp", None),
            P(None, None, "fsdp", None),
            P("replica"),
        ),
        out_specs=(
            P(("replica", "fsdp"), None),
            P(None, None, "fsdp", None),
            P(None, None, "fsdp", None),
        ),
        check_vma=False,
    )
```
